128 devices in a mesh: clip: 4 (over y), tm: 32 (over x, z, core).
Axes of the slice: x: 4, y: 4, z: 4, core: 2. Of those that a mesh axis runs over, the one named last changes fastest.
Arguments:
- latent: bfloat16 [8, 512, 64], P('clip', 'tm'), may hold values from -6 to 6
- dest: int32 [8], replicated, may hold values from 0 to 7, each once
- lengths: int32 [8], replicated, may hold values from 128 to 512, as said below
- input_conv_weight: bfloat16 [7, 64, 2048], replicated, may hold values from -0.25 to 0.25
- snake_entry_frequency: float32 [2048], replicated, may hold values from 0.5 to 2
- upsample_weight: bfloat16 [2048, 16, 1024], P('tm', None, 'clip'), may hold values from -0.09375 to 0.09375
- snake_unit_frequency: float32 [2, 2, 1024], P(None, None, 'clip'), may hold values from 0.5 to 2
- dilated_conv_weight: bfloat16 [2, 7, 1024, 1024], P(None, None, 'tm', 'clip'), may hold values from -0.0625 to 0.0625
- pointwise_conv_weight: bfloat16 [2, 1024, 1024], P(None, 'tm', 'clip'), may hold values from -0.1875 to 0.1875
Outputs:
- decoded: bfloat16 [8, 4096, 1024], P(None, 'tm', 'clip')
- energy: float32 [8, 1024], P(None, ('clip', 'tm'))
The draws below stay inside these ranges and needn't reach their ends.
Inputs may be any that keep to these rules, and one draw needn't show every extreme that they name: `lengths`: at least one slot has all 512 frames live; no slot has fewer than 128.
All inputs are finite; a program needn't handle non-finite values.
Results may differ from the reference program's by a relative error of at most 0.012.
Values may be sent and summed in bfloat16 or wider, within the bound.
No kernel may reach another device: no remote copies, remote signals or barrier semaphores. Data moves between devices by JAX's collectives and lax.ppermute only.
A program may use at most 128 MiB of HBM per device.

```python
import math
import jax
import jax.numpy as jnp

LATENT = 64
C0 = 2048
SECTION_CHANNELS = 1024
KERNEL_TAPS = 7
UPK = 16
RESIDUAL_UNITS = 2
CLIPS = 8
FRAMES = 512


def draw_lengths(key, part):
    key = jax.random.fold_in(key, 11)
    first_key, second_key = jax.random.split(key)
    base = jax.random.randint(first_key, (CLIPS,), FRAMES // 4, FRAMES + 1)
    full_slot = jax.random.randint(second_key, (), 0, CLIPS)
    return jnp.where(jnp.arange(CLIPS) == full_slot, FRAMES, base).astype(jnp.int32)


def block_scale(own_key, extent, cuts, smallest, high):
    def one(dim, shards_of):
        heights = jax.random.uniform(jax.random.fold_in(jax.random.fold_in(own_key, 6), dim), (shards_of,), jnp.float32, smallest / len(cuts), high / len(cuts))
        return jnp.repeat(jnp.exp(heights), extent[dim] // shards_of).reshape((-1,) + (1,) * (len(extent) - dim - 1))

    factor_of = one(*cuts[0])
    for cut in cuts[1:]:
        factor_of = factor_of * one(*cut)
    return factor_of


def noise(own_key, dims, width, bound, cuts=(), dtype=jnp.bfloat16):
    entries = jax.random.normal(own_key, dims, jnp.float32) * width
    if len(cuts) > 0:
        entries = block_scale(own_key, dims, cuts, -0.22, 0.18) * entries
    return jnp.clip(entries, min=-bound, max=bound).astype(dtype)


def setup_inputs(seed: int = 0) -> dict:
    arg_keys = jax.random.split(jax.random.key(seed), 10)
    latent = noise(arg_keys[0], (CLIPS, FRAMES, LATENT), 1.0, 6.0, ((0, 4), (1, 32)))
    dest = jax.random.permutation(arg_keys[1], CLIPS).astype(jnp.int32)
    lengths = draw_lengths(jax.random.fold_in(arg_keys[9], 71), 0)
    input_conv_weight = noise(arg_keys[3], (KERNEL_TAPS, LATENT, C0), (KERNEL_TAPS * LATENT) ** -0.5, 0.25)
    snake_entry_frequency = jnp.clip(jnp.exp(jax.random.uniform(arg_keys[4], (C0,), jnp.float32, math.log(0.5), math.log(2.0))), 0.5, 2.0)
    upsample_weight = noise(arg_keys[5], (C0, UPK, SECTION_CHANNELS), (2 * C0) ** -0.5, 0.09375, ((0, 32), (2, 4)))
    snake_unit_frequency = jnp.clip(jnp.exp(math.log(2.0) - 1.3862944 * jax.random.uniform(arg_keys[6], (RESIDUAL_UNITS, 2, SECTION_CHANNELS), jnp.float32) ** block_scale(arg_keys[6], (RESIDUAL_UNITS, 2, SECTION_CHANNELS), ((2, 4),), -0.2, 0.2)), 0.5, 2.0)
    dilated_conv_weight = noise(arg_keys[7], (RESIDUAL_UNITS, KERNEL_TAPS, SECTION_CHANNELS, SECTION_CHANNELS), (KERNEL_TAPS * SECTION_CHANNELS) ** -0.5, 0.0625, ((2, 32), (3, 4)))
    pointwise_conv_weight = noise(arg_keys[8], (RESIDUAL_UNITS, SECTION_CHANNELS, SECTION_CHANNELS), SECTION_CHANNELS ** -0.5, 0.1875, ((1, 32), (2, 4)))
    return {"latent": latent, "dest": dest, "lengths": lengths, "input_conv_weight": input_conv_weight, "snake_entry_frequency": snake_entry_frequency, "upsample_weight": upsample_weight, "snake_unit_frequency": snake_unit_frequency, "dilated_conv_weight": dilated_conv_weight, "pointwise_conv_weight": pointwise_conv_weight}


def snake(value, alpha):
    return value + jnp.sin(alpha * value) ** 2 / alpha


def reference(latent, dest, lengths, input_conv_weight, snake_entry_frequency, upsample_weight, snake_unit_frequency, dilated_conv_weight, pointwise_conv_weight):
    frames = latent.shape[1]
    c0 = upsample_weight.shape[0]
    upk = upsample_weight.shape[1]
    c1 = upsample_weight.shape[2]
    quarter = upk // 4
    stride = upk // 2
    sample_rows = stride * frames
    picked = jnp.take(latent, dest, axis=0)
    live = jnp.arange(frames)[None, :] < lengths[:, None]
    picked = jnp.where(live[:, :, None], picked, jnp.zeros_like(picked))
    outs_dec = []
    outs_energy = []
    for slot in range(picked.shape[0]):
        padded = jnp.pad(picked[slot], ((3, 3), (0, 0)))
        pre = jnp.zeros((frames, c0), jnp.float32)
        for kernel_tap in range(input_conv_weight.shape[0]):
            pre = pre + jnp.dot(padded[kernel_tap:kernel_tap + frames], input_conv_weight[kernel_tap], preferred_element_type=jnp.float32)
        s_zero = snake(pre, snake_entry_frequency).astype(jnp.bfloat16)
        prod = jnp.dot(s_zero, upsample_weight.reshape(c0, upk * c1), preferred_element_type=jnp.float32).reshape(frames, upk, c1)
        blank = jnp.zeros((1, upk, c1), jnp.float32)
        before = jnp.concatenate([blank, prod[:-1]], axis=0)
        after = jnp.concatenate([prod[1:], blank], axis=0)
        first = prod[:, quarter:2 * quarter] + before[:, 3 * quarter:4 * quarter]
        second = prod[:, 2 * quarter:3 * quarter] + after[:, 0:quarter]
        state = jnp.concatenate([first, second], axis=1).reshape(sample_rows, c1)
        for residual_unit in range(dilated_conv_weight.shape[0]):
            dilation_factor = 3 ** residual_unit
            snake_activation = snake(state, snake_unit_frequency[residual_unit, 0]).astype(jnp.bfloat16)
            snake_activation = jnp.pad(snake_activation, ((3 * dilation_factor, 3 * dilation_factor), (0, 0)))
            inner_signal = jnp.zeros((sample_rows, c1), jnp.float32)
            for kernel_tap in range(dilated_conv_weight.shape[1]):
                inner_signal = inner_signal + jnp.dot(snake_activation[kernel_tap * dilation_factor:kernel_tap * dilation_factor + sample_rows], dilated_conv_weight[residual_unit, kernel_tap], preferred_element_type=jnp.float32)
            branch = snake(inner_signal, snake_unit_frequency[residual_unit, 1]).astype(jnp.bfloat16)
            state = state + jnp.dot(branch, pointwise_conv_weight[residual_unit], preferred_element_type=jnp.float32)
        outs_dec.append(state.astype(jnp.bfloat16))
        valid = jnp.arange(sample_rows) < stride * lengths[slot]
        total = jnp.sum(jnp.where(valid[:, None], state * state, jnp.float32(0.0)), axis=0)
        count = (stride * lengths[slot]).astype(jnp.float32)
        outs_energy.append(jnp.log(total / count + 1e-6))
    return jnp.stack(outs_dec), jnp.stack(outs_energy)
```

```python
import functools
import math

import jax
import jax.numpy as jnp
from jax import lax
from jax.experimental import pallas as pl
from jax.experimental.pallas import tpu as pltpu
from jax.sharding import Mesh
from jax.sharding import PartitionSpec as P

BF = jnp.bfloat16
F32 = jnp.float32
SIN2 = (
    9.869603157043457,
    -32.469581604003906,
    42.72538375854492,
    -30.085952758789062,
    12.990730285644531,
    -3.2729458808898926,
)
ROW_CHUNK = 256
EDGE = 2
VMEM = 56 * 1024 * 1024


def snake(value, turns, inverse):
    u = value * turns
    r = u - jnp.round(u)
    z = r * r
    p = jnp.full_like(z, SIN2[-1])
    for coefficient in SIN2[-2::-1]:
        p = p * z + coefficient
    return value + (p * z) * inverse


def entry_kernel(lat_ref, w_ref, freq_ref, s0_ref):
    width = 256
    for n in range(s0_ref.shape[1] // width):
        cols = pl.ds(n * width, width)
        pre = jnp.dot(lat_ref[...], w_ref[:, cols], preferred_element_type=F32)
        s0_ref[:, cols] = snake(pre, freq_ref[0:1, cols], freq_ref[1:2, cols]).astype(BF)


def upsample_kernel(slots, flag_ref, s0_ref, own_ref, other_ref, out_ref, w_s, prod_s, x_s):
    step, steps = pl.program_id(0), pl.num_programs(0)
    groups, rows, cols = own_ref.shape
    half = cols // 2

    @pl.when(step == 0)
    def _():
        @pl.when(flag_ref[0] == 0)
        def _():
            for g in range(groups):
                w_s[pl.ds(2 * g * rows, rows), :] = own_ref[g]
                w_s[pl.ds((2 * g + 1) * rows, rows), :] = other_ref[g]

        @pl.when(flag_ref[0] != 0)
        def _():
            for g in range(groups):
                w_s[pl.ds(2 * g * rows, rows), :] = other_ref[g]
                w_s[pl.ds((2 * g + 1) * rows, rows), :] = own_ref[g]

        prod_s[0:8, :] = jnp.zeros((8, cols), F32)
        prod_s[prod_s.shape[0] - 8 :, :] = jnp.zeros((8, cols), F32)

    chunk = s0_ref.shape[0]
    at = pl.multiple_of(8 + step * chunk, 8)
    prod_s[pl.ds(at, chunk), :] = jnp.dot(s0_ref[...], w_s[...], preferred_element_type=F32)

    @pl.when(step == steps - 1)
    def _():
        total = prod_s.shape[0] - 16
        pad = EDGE * slots
        x_s[0:pad, :] = jnp.zeros((pad, half), F32)
        x_s[x_s.shape[0] - pad :, :] = jnp.zeros((pad, half), F32)
        low = flag_ref[1] == 0
        for r in range(0, total, chunk):
            centre = prod_s[8 + r : 8 + r + chunk, :half]
            before = prod_s[8 - slots + r : 8 - slots + r + chunk, half:]
            after = prod_s[8 + slots + r : 8 + slots + r + chunk, half:]
            x_s[pad + r : pad + r + chunk, :] = centre + jnp.where(low, before, after)
        window = out_ref.shape[1]
        own = window - 2 * pad
        for d in range(out_ref.shape[0]):
            out_ref[d] = x_s[d * own : d * own + window, :].astype(BF)


def taps_to_shift(phases, dilation, tap, phase):
    moved = phase + dilation * (tap - 3)
    return moved % phases, moved // phases


def fill(act_s, lhs_s, dilation, slots, first, rows):
    taps, phases = lhs_s.shape[0], act_s.shape[0]
    wanted = {}
    for t in range(taps):
        for s in range(phases):
            wanted.setdefault(taps_to_shift(phases, dilation, t, s), []).append((t, s))
    for (source, shift), uses in sorted(wanted.items()):
        at = 8 + first + shift * slots
        piece = act_s[source, at : at + rows, :].astype(BF)
        for t, s in uses:
            lhs_s[t, s * rows : (s + 1) * rows, :] = piece


def conv(lhs_s, w_ref, acc_s):
    taps = lhs_s.shape[0]
    depth = lhs_s.shape[2]

    def one(t):
        w = w_ref[0, :, t].reshape(depth, w_ref.shape[-1])
        return jnp.dot(lhs_s[t], w, preferred_element_type=F32)

    acc_s[...] = one(0)

    @pl.loop(1, taps)
    def _(t):
        acc_s[...] += one(t)


def unit0_kernel(slots, x_ref, w_ref, pw_ref, freq_ref, out_ref, act_s, lhs_s, acc_s, b_s):
    y = pl.program_id(0)
    groups, phases, halves, rows, lanes = x_ref.shape

    @pl.when(y == 0)
    def _():
        for s in range(phases):
            act_s[s, 0:8, :] = jnp.zeros((8, act_s.shape[2]), F32)
            act_s[s, 8 + rows :, :] = jnp.zeros((8, act_s.shape[2]), F32)
            for g in range(groups):
                for h in range(halves):
                    cols = slice((g * halves + h) * lanes, (g * halves + h + 1) * lanes)
                    v = x_ref[g, s, h].astype(F32)
                    act_s[s, 8 : 8 + rows, cols] = snake(v, freq_ref[0:1, cols], freq_ref[1:2, cols])
        fill(act_s, lhs_s, 1, slots, 0, rows)

    conv(lhs_s, w_ref, acc_s)
    width = acc_s.shape[1]
    cols = pl.ds(pl.multiple_of(y * width, width), width)
    b_s[:, cols] = snake(acc_s[...], freq_ref[2:3, cols], freq_ref[3:4, cols]).astype(BF)

    @pl.when(y == groups - 1)
    def _():
        for g in range(groups):
            w = pw_ref[g].reshape(b_s.shape[1], width)
            acc_s[...] = jnp.dot(b_s[...], w, preferred_element_type=F32)
            for s in range(phases):
                for h in range(halves):
                    at = slice(s * rows, (s + 1) * rows)
                    out_ref[g, at, h * lanes : (h + 1) * lanes] = (
                        acc_s[at, h * lanes : (h + 1) * lanes] + x_ref[g, s, h].astype(F32)
                    )


def unit1_kernel(
    slots, x_ref, w_ref, pw_ref, freq_ref, inside_ref, live_ref, dec_ref, energy_ref, act_s, lhs_s, acc_s, b_s, t_s, o_s
):
    y = pl.program_id(0)
    groups, all_rows, width = x_ref.shape
    phases = act_s.shape[0]
    rows = all_rows // phases
    first = EDGE * slots
    kept = rows - 2 * first
    frames = kept // slots

    @pl.when(y == 0)
    def _():
        for s in range(phases):
            act_s[s, 0:8, :] = jnp.zeros((8, act_s.shape[2]), F32)
            act_s[s, 8 + rows :, :] = jnp.zeros((8, act_s.shape[2]), F32)
            for g in range(groups):
                cols = slice(g * width, (g + 1) * width)
                v = x_ref[g, s * rows : (s + 1) * rows, :]
                act_s[s, 8 : 8 + rows, cols] = (
                    snake(v, freq_ref[0:1, cols], freq_ref[1:2, cols]) * inside_ref[...]
                )
        fill(act_s, lhs_s, 3, slots, first, kept)

    conv(lhs_s, w_ref, acc_s)
    cols = pl.ds(pl.multiple_of(y * width, width), width)
    b_s[:, cols] = snake(acc_s[...], freq_ref[2:3, cols], freq_ref[3:4, cols]).astype(BF)

    @pl.when(y == groups - 1)
    def _():
        for g in range(groups):
            w = pw_ref[g].reshape(b_s.shape[1], width)
            acc_s[...] = jnp.dot(b_s[...], w, preferred_element_type=F32)
            for s in range(phases):
                at = s * rows + first
                acc_s[s * kept : (s + 1) * kept, :] += x_ref[g, at : at + kept, :]
            live = live_ref[...]
            squares = jnp.zeros((kept, width), F32)
            for s in range(phases):
                v = acc_s[s * kept : (s + 1) * kept, :]
                squares += v * v * live
            energy_ref[:, g * width : (g + 1) * width] = squares
            for h in range(width // 128):
                lanes = slice(h * 128, (h + 1) * 128)
                for s in range(phases):
                    t_s[...] = acc_s[s * kept : (s + 1) * kept, lanes]
                    for k in range(slots):
                        o_s[pl.ds(k * frames * phases + s, frames, stride=phases), :] = t_s[
                            pl.ds(k, frames, stride=slots), :
                        ]
                for k in range(slots):
                    dec_ref[g, k, :, lanes] = o_s[k * frames * phases : (k + 1) * frames * phases, :].astype(BF)


def cost(flops, moved):
    return pl.CostEstimate(flops=flops, bytes_accessed=moved, transcendentals=0)


def run_entry(lat, w, freq):
    rows, depth = lat.shape
    c0 = w.shape[1]
    return pl.pallas_call(
        entry_kernel,
        grid=(rows // ROW_CHUNK,),
        in_specs=[
            pl.BlockSpec((ROW_CHUNK, depth), lambda i: (i, 0)),
            pl.BlockSpec((depth, c0), lambda i: (0, 0)),
            pl.BlockSpec((2, c0), lambda i: (0, 0)),
        ],
        out_specs=pl.BlockSpec((ROW_CHUNK, c0), lambda i: (i, 0)),
        out_shape=jax.ShapeDtypeStruct((rows, c0), BF),
        compiler_params=pltpu.CompilerParams(vmem_limit_bytes=VMEM),
        cost_estimate=cost(2 * rows * depth * c0, 2 * rows * c0),
        name="entry",
    )(lat, w, freq)


def run_upsample(flags, s0, own, other, slots, chips):
    rows, c0 = s0.shape
    cols = own.shape[2]
    half = cols // 2
    pad = EDGE * slots
    window = rows // chips + 2 * pad
    whole = pl.BlockSpec(own.shape, lambda i: (0, 0, 0))
    return pl.pallas_call(
        functools.partial(upsample_kernel, slots),
        grid=(rows // ROW_CHUNK,),
        in_specs=[
            pl.BlockSpec(memory_space=pltpu.SMEM),
            pl.BlockSpec((ROW_CHUNK, c0), lambda i: (i, 0)),
            whole,
            whole,
        ],
        out_specs=pl.BlockSpec((chips, window, half), lambda i: (0, 0, 0)),
        out_shape=jax.ShapeDtypeStruct((chips, window, half), BF),
        scratch_shapes=[
            pltpu.VMEM((c0, cols), BF),
            pltpu.VMEM((rows + 16, cols), F32),
            pltpu.VMEM((rows + 2 * pad, half), F32),
        ],
        compiler_params=pltpu.CompilerParams(vmem_limit_bytes=VMEM),
        cost_estimate=cost(2 * rows * c0 * cols, 2 * rows * c0),
        name="upsample",
    )(flags, s0, own, other)


def weight_specs(weights, unit):
    groups, shards, _, kinds, rows, width = weights.shape
    return [
        pl.BlockSpec((1, shards, None, kinds, rows, width), lambda i: (i, 0, unit, 0, 0, 0)),
        pl.BlockSpec((groups, shards, None, None, rows, width), lambda i: (0, 0, unit, kinds - 1, 0, 0)),
    ]


def run_unit0(x, weights, freq, slots):
    groups, phases, halves, rows, lanes = x.shape
    taps = weights.shape[3] - 1
    channels, width = groups * halves * lanes, halves * lanes
    m = phases * rows
    return pl.pallas_call(
        functools.partial(unit0_kernel, slots),
        grid=(groups,),
        in_specs=[
            pl.BlockSpec(x.shape, lambda i: (0, 0, 0, 0, 0)),
            *weight_specs(weights, 0),
            pl.BlockSpec(freq.shape, lambda i: (0, 0)),
        ],
        out_specs=pl.BlockSpec((groups, m, width), lambda i: (0, 0, 0)),
        out_shape=jax.ShapeDtypeStruct((groups, m, width), F32),
        scratch_shapes=[
            pltpu.VMEM((phases, rows + 16, channels), F32),
            pltpu.VMEM((taps, m, channels), BF),
            pltpu.VMEM((m, width), F32),
            pltpu.VMEM((m, channels), BF),
        ],
        compiler_params=pltpu.CompilerParams(vmem_limit_bytes=VMEM),
        cost_estimate=cost(2 * m * (taps + 1) * channels * channels, weights.size),
        name="unit0",
    )(x, weights, weights, freq)


def run_unit1(x, weights, freq, inside, live, slots, phases):
    groups, all_rows, width = x.shape
    rows = all_rows // phases
    kept = rows - 2 * EDGE * slots
    taps = weights.shape[3] - 1
    channels = groups * width
    m = phases * kept
    samples = m // slots
    return pl.pallas_call(
        functools.partial(unit1_kernel, slots),
        grid=(groups,),
        in_specs=[
            pl.BlockSpec(x.shape, lambda i: (0, 0, 0)),
            *weight_specs(weights, 1),
            pl.BlockSpec(freq.shape, lambda i: (0, 0)),
            pl.BlockSpec(inside.shape, lambda i: (0, 0)),
            pl.BlockSpec(live.shape, lambda i: (0, 0)),
        ],
        out_specs=[
            pl.BlockSpec((groups, slots, samples, width), lambda i: (0, 0, 0, 0)),
            pl.BlockSpec((kept, channels), lambda i: (0, 0)),
        ],
        out_shape=[
            jax.ShapeDtypeStruct((groups, slots, samples, width), BF),
            jax.ShapeDtypeStruct((kept, channels), F32),
        ],
        scratch_shapes=[
            pltpu.VMEM((phases, rows + 16, channels), F32),
            pltpu.VMEM((taps, m, channels), BF),
            pltpu.VMEM((m, width), F32),
            pltpu.VMEM((m, channels), BF),
            pltpu.VMEM((kept, 128), F32),
            pltpu.VMEM((m, 128), F32),
        ],
        compiler_params=pltpu.CompilerParams(vmem_limit_bytes=VMEM),
        cost_estimate=cost(2 * m * (taps + 1) * channels * channels, weights.size),
        name="unit1",
    )(x, weights, weights, freq, inside, live)


def freq_rows(alpha):
    return jnp.stack([alpha / math.pi, 1.0 / alpha], axis=-2)


def body(
    latent,
    dest,
    lengths,
    input_conv_weight,
    snake_entry_frequency,
    upsample_weight,
    snake_unit_frequency,
    dilated_conv_weight,
    pointwise_conv_weight,
):
    everyone = ("y", "x", "z", "c")
    blocks = ("x", "z", "y")
    ny, nx, nz, nc = (lax.axis_size(a) for a in everyone)
    iy, ix, iz, ic = (lax.axis_index(a) for a in everyone)
    chips = ny * nx * nz
    here_clips, here_frames, width_in = latent.shape
    clips = dest.shape[0]
    frames = here_frames * nx * nz * nc
    slots = clips // nc
    own_frames = frames // chips
    units, taps = dilated_conv_weight.shape[:2]
    upk, c1_local = upsample_weight.shape[1:]
    phases = upk // 2
    halves = nx * nz // phases
    lanes = c1_local // halves
    first_slot = ic * slots

    weights = jnp.concatenate([dilated_conv_weight, pointwise_conv_weight[:, None]], axis=1)
    shape = weights.shape
    weights = lax.all_gather(weights.reshape(-1, *shape[2:]), everyone, axis=0, tiled=True)
    weights = weights.reshape(ny, nx * nz * nc, *shape)

    packed = latent.transpose(1, 0, 2).reshape(here_frames, here_clips * width_in)
    packed = jnp.broadcast_to(packed[None], (ny * nx * nz * nc,) + packed.shape)
    packed = lax.all_to_all(packed, everyone, 0, 0, tiled=True)
    order = []
    for s in range(phases):
        near = s + phases // 2
        far = s + 3 * phases // 2 if s < phases // 2 else s - phases // 2
        order += [near, far]
    up = upsample_weight.transpose(1, 0, 2)
    up = jnp.stack([up[q] for q in order]).reshape(phases, 2, -1, halves, lanes)
    up = up.transpose(0, 3, 2, 1, 4).reshape(phases * halves, -1, 2 * lanes)
    up, packed = lax.optimization_barrier((up, packed))
    packed = packed.reshape(ny, frames, here_clips, width_in).transpose(0, 2, 1, 3)
    packed = packed.reshape(clips, frames, width_in)
    my_dest = lax.dynamic_slice_in_dim(dest, first_slot, slots)
    my_lengths = lax.dynamic_slice_in_dim(lengths, first_slot, slots)
    picked = jnp.take(packed, my_dest, axis=0)
    live = jnp.arange(frames)[None, :] < my_lengths[:, None]
    picked = jnp.where(live[:, :, None], picked, jnp.zeros_like(picked)).transpose(1, 0, 2)
    reach = input_conv_weight.shape[0] // 2
    picked = jnp.pad(picked, ((reach, reach), (0, 0), (0, 0)))
    picked = jnp.concatenate([picked[t : t + frames] for t in range(2 * reach + 1)], axis=2)
    picked = picked.reshape(frames * slots, -1)
    own = lax.all_to_all(up, ("x", "z"), 0, 0, tiled=True)
    other = lax.ppermute(own, "c", [(i, nc - 1 - i) for i in range(nc)])

    w_in = input_conv_weight.reshape(-1, input_conv_weight.shape[2])
    s0 = run_entry(picked, w_in, freq_rows(snake_entry_frequency))
    flags = jnp.stack([ic, (ix * nz + iz) // (phases // 2 * halves)]).astype(jnp.int32)
    x = run_upsample(flags, s0, own, other, slots, chips)
    x = lax.all_to_all(x, blocks, 0, 0, tiled=True)
    window = x.shape[1]
    x = x.reshape(phases, halves, ny, window, lanes).transpose(2, 0, 1, 3, 4)

    freq = freq_rows(snake_unit_frequency).reshape(1, -1, c1_local)
    freq = lax.all_to_all(jnp.broadcast_to(freq, (ny,) + freq.shape[1:]), "y", 0, 0, tiled=True)
    freq = freq.transpose(1, 0, 2).reshape(units, -1, ny * c1_local)

    x = run_unit0(x, weights, freq[0], slots)

    block = (ix * nz + iz) * ny + iy
    at = block * own_frames - EDGE + jnp.arange(own_frames + 2 * EDGE)
    inside = ((at >= 0) & (at < frames)).astype(F32)
    inside = jnp.broadcast_to(jnp.repeat(inside, slots)[:, None], (window, c1_local))
    at = at[EDGE:-EDGE]
    live = (at[:, None] < my_lengths[None, :]).astype(F32).reshape(-1)
    live = jnp.broadcast_to(live[:, None], (own_frames * slots, c1_local))
    decoded, squares = run_unit1(x, weights, freq[1], inside, live, slots, phases)

    decoded = lax.all_to_all(decoded, "y", 0, 0, tiled=True)
    part = ny // nc
    kept = lax.dynamic_slice_in_dim(decoded, ic * part, part)
    sent = lax.dynamic_slice_in_dim(decoded, (nc - 1 - ic) * part, part)
    came = lax.ppermute(sent, "c", [(i, nc - 1 - i) for i in range(nc)])
    low = ic == 0
    decoded = jnp.stack([jnp.where(low, kept, came), jnp.where(low, came, kept)])
    samples = part * decoded.shape[3]
    decoded = decoded.transpose(0, 2, 1, 3, 4).reshape(clips, samples, c1_local)

    squares = squares.reshape(own_frames, slots, -1).sum(axis=0)
    squares = squares.reshape(slots, ny * nx * nz * nc, -1).transpose(1, 0, 2)
    squares = lax.all_to_all(squares, everyone, 0, 0, tiled=True)
    squares = squares.reshape(chips, clips, -1).sum(axis=0)
    count = (phases * lengths[:, None]).astype(F32)
    energy = jnp.log(squares / count + 1e-06)
    return decoded, energy


def solution(mesh):
    ny = mesh.shape["clip"]
    side = 4
    fine = Mesh(mesh.devices.reshape(ny, side, side, 2), ("y", "x", "z", "c"))
    tm = ("x", "z", "c")
    in_specs = (
        P("y", tm, None),
        P(),
        P(),
        P(),
        P(),
        P(tm, None, "y"),
        P(None, None, "y"),
        P(None, None, tm, "y"),
        P(None, tm, "y"),
    )
    out_specs = (P(None, tm, "y"), P(None, ("y",) + tm))
    return jax.shard_map(body, mesh=fine, in_specs=in_specs, out_specs=out_specs, check_vma=False)
```

```python
import functools
import math

import jax
import jax.numpy as jnp
from jax import lax
from jax.experimental import pallas as pl
from jax.experimental.pallas import tpu as pltpu
from jax.sharding import Mesh
from jax.sharding import PartitionSpec as P

BF = jnp.bfloat16
F32 = jnp.float32
SIN2 = (
    9.869603157043457,
    -32.469581604003906,
    42.72538375854492,
    -30.085952758789062,
    12.990730285644531,
    -3.2729458808898926,
)
ROW_CHUNK = 512
EDGE = 2
VMEM = 60 * 1024 * 1024


def snake(value, turns, inverse):
    u = value * turns
    r = u - jnp.round(u)
    z = r * r
    p = jnp.full_like(z, SIN2[-1])
    for coefficient in SIN2[-2::-1]:
        p = p * z + coefficient
    return value + (p * z) * inverse


def front_kernel(slots, info_ref, lat_ref, w_in_ref, freq_ref, own_ref, other_ref, out_ref, w_s, one_s, two_s, prod_s, x_s):
    step, steps = pl.program_id(0), pl.num_programs(0)
    groups, depth, cols = own_ref.shape
    half = cols // 2
    _, frames, lanes = lat_ref.shape
    width = lanes // 2
    reach = w_in_ref.shape[0] // width // 2
    rows = frames * slots

    @pl.when(step == 0)
    def _():
        column = lax.broadcasted_iota(jnp.int32, (frames, lanes), 1)
        frame = lax.broadcasted_iota(jnp.int32, (frames, lanes), 0)
        edge = reach * slots
        one_s[0:edge, :] = jnp.zeros((edge, lanes), F32)
        one_s[edge + rows :, :] = jnp.zeros((one_s.shape[0] - edge - rows, lanes), F32)
        for k in range(slots):
            clip = info_ref[2 + k]
            v = lat_ref[lax.div(clip, 2)].astype(F32)
            v = jnp.where(lax.rem(clip, 2) == 1, pltpu.roll(v, width, 1), v)
            keep = (column < width) & (frame < info_ref[2 + slots + k])
            one_s[pl.ds(edge + k, frames, stride=slots), :] = jnp.where(keep, v, 0.0)
        total = two_s.shape[0]
        for r in range(0, total, ROW_CHUNK):
            size = min(ROW_CHUNK, total - r)
            after = pltpu.roll(one_s[r + slots : r + slots + size, :], width, 1)
            two_s[r : r + size, :] = one_s[r : r + size, :] + after

        first, second = (own_ref, other_ref), (other_ref, own_ref)
        for core, pair in enumerate((first, second)):

            @pl.when(info_ref[0] == core)
            def _(pair=pair):
                for g in range(groups):
                    for c in range(2):
                        w_s[(2 * g + c) * depth : (2 * g + c + 1) * depth, :] = pair[c][g]

        prod_s[0:8, :] = jnp.zeros((8, cols), F32)
        prod_s[prod_s.shape[0] - 8 :, :] = jnp.zeros((8, cols), F32)

    at = pl.multiple_of(step * ROW_CHUNK, ROW_CHUNK)
    taps = 2 * reach + 1
    lhs = []
    for t in range(0, taps, 2):
        v = two_s[pl.ds(pl.multiple_of(at + t * slots, 8), ROW_CHUNK), :].astype(BF)
        lhs.append(v if t + 1 < taps else v[:, :width])
    lhs = jnp.concatenate(lhs, axis=1)
    total = None
    block = 512
    for n in range(w_in_ref.shape[1] // block):
        part = slice(n * block, (n + 1) * block)
        pre = jnp.dot(lhs, w_in_ref[:, part], preferred_element_type=F32)
        s0 = snake(pre, freq_ref[0:1, part], freq_ref[1:2, part]).astype(BF)
        term = jnp.dot(s0, w_s[part, :], preferred_element_type=F32)
        total = term if total is None else total + term
    prod_s[pl.ds(pl.multiple_of(8 + at, 8), ROW_CHUNK), :] = total

    @pl.when(step == steps - 1)
    def _():
        pad = EDGE * slots
        x_s[0:pad, :] = jnp.zeros((pad, half), F32)
        x_s[x_s.shape[0] - pad :, :] = jnp.zeros((pad, half), F32)
        low = info_ref[1] == 0
        for r in range(0, rows, ROW_CHUNK):
            centre = prod_s[8 + r : 8 + r + ROW_CHUNK, :half]
            before = prod_s[8 - slots + r : 8 - slots + r + ROW_CHUNK, half:]
            after = prod_s[8 + slots + r : 8 + slots + r + ROW_CHUNK, half:]
            x_s[pad + r : pad + r + ROW_CHUNK, :] = centre + jnp.where(low, before, after)
        window = out_ref.shape[1]
        kept = window - 2 * pad
        for d in range(out_ref.shape[0]):
            out_ref[d] = x_s[d * kept : d * kept + window, :].astype(BF)


def activate_kernel(slots, x_ref, freq_ref, out_ref, act_s):
    phases, halves, groups, rows, lanes = x_ref.shape
    for s in range(phases):
        act_s[s, 0:8, :] = jnp.zeros((8, act_s.shape[2]), F32)
        act_s[s, 8 + rows :, :] = jnp.zeros((8, act_s.shape[2]), F32)
        for g in range(groups):
            for h in range(halves):
                cols = slice((g * halves + h) * lanes, (g * halves + h + 1) * lanes)
                v = x_ref[s, h, g].astype(F32)
                act_s[s, 8 : 8 + rows, cols] = snake(v, freq_ref[0, 0:1, cols], freq_ref[0, 1:2, cols])
    reach = (out_ref.shape[0] - phases) // 2
    for i in range(out_ref.shape[0]):
        n = i - reach
        at = 8 + n // phases * slots
        out_ref[i] = act_s[n % phases, at : at + rows, :].astype(BF)


def units_kernel(
    slots,
    info_ref,
    a0_ref,
    x_ref,
    freq_ref,
    w_ref,
    *refs,
):
    phases, halves, groups, rows, lanes = x_ref.shape
    dec_refs = refs[:groups]
    near_ref, far_ref, w_s, p_s, act_s, a1_s, x1_s, acc_s, b_s, t_s, o_s, w_sem, p_sem = refs[groups:]
    taps = w_s.shape[2]
    width = halves * lanes
    channels = groups * width
    first = EDGE * slots
    kept = rows - 2 * first
    frames = kept // slots
    units = w_sem.shape[0] // groups

    def fetch(unit):
        for g in range(groups):
            i = unit * groups + g
            yield pltpu.make_async_copy(w_ref.at[g, :, unit * taps : (unit + 1) * taps], w_s.at[i], w_sem.at[i])
        yield pltpu.make_async_copy(w_ref.at[:, :, units * taps + unit], p_s.at[unit], p_sem.at[unit])

    for copy in list(fetch(0))[: groups // 2]:
        copy.start()

    row = lax.broadcasted_iota(jnp.int32, (rows, lanes), 0)
    at = info_ref[0] - EDGE + (row >> (slots.bit_length() - 1))
    inside = jnp.where((at >= 0) & (at < info_ref[1]), 1.0, 0.0).astype(F32)
    row = lax.broadcasted_iota(jnp.int32, (kept, lanes), 0)
    at = info_ref[0] + (row >> (slots.bit_length() - 1))
    slot = row & (slots - 1)
    limit = jnp.zeros((kept, lanes), jnp.int32)
    for k in range(slots):
        limit = jnp.where(slot == k, info_ref[4 + k], limit)
    live = jnp.where(at < limit, 1.0, 0.0).astype(F32)

    for s in range(phases):
        act_s[s, 0:8, :] = jnp.zeros((8, channels), F32)
        act_s[s, 8 + rows :, :] = jnp.zeros((8, channels), F32)

    for unit in range(units):
        a_ref = a0_ref if unit == 0 else a1_s
        dilation = 3**unit
        m = phases * a_ref.shape[1]
        copies = list(fetch(unit))
        ahead = list(fetch(unit + 1)) if unit + 1 < units else []
        split = groups // 2 if unit == 0 else len(copies)
        for copy in copies[:split]:
            copy.wait()
        for copy in copies[split:] + ([] if unit == 0 else ahead):
            copy.start()
        for g in range(groups):
            if unit == 0 and g == split:
                for copy in copies[split:]:
                    copy.wait()
                for copy in ahead:
                    copy.start()
            total = None
            for t in range(taps):
                lhs = a_ref[dilation * t : dilation * t + phases].reshape(m, channels)
                rhs = w_s[unit * groups + g, :, t].reshape(channels, width)
                term = jnp.dot(lhs, rhs, preferred_element_type=F32)
                total = term if total is None else total + term
            acc_s[g % 2, 0:m] = total
            cols = slice(g * width, (g + 1) * width)
            b_s[0:m, cols] = snake(
                acc_s[g % 2, 0:m], freq_ref[unit, 2:3, cols], freq_ref[unit, 3:4, cols]
            ).astype(BF)
        if unit == 0:
            for g in range(groups):
                acc = acc_s.at[g % 2]
                acc[0:m] = jnp.dot(b_s[0:m], p_s[unit, g].reshape(channels, width), preferred_element_type=F32)
                for s in range(phases):
                    for h in range(halves):
                        cols = slice(g * width + h * lanes, g * width + (h + 1) * lanes)
                        v = acc[s * rows : (s + 1) * rows, h * lanes : (h + 1) * lanes]
                        v = v + x_ref[s, h, g].astype(F32)
                        x1_s[s, :, cols] = v[first : first + kept]
                        act_s[s, 8 : 8 + rows, cols] = (
                            snake(v, freq_ref[1, 0:1, cols], freq_ref[1, 1:2, cols]) * inside
                        )
            reach = (a1_s.shape[0] - phases) // 2
            for i in range(a1_s.shape[0]):
                n = i - reach
                at = 8 + first + n // phases * slots
                a1_s[i] = act_s[n % phases, at : at + kept, :].astype(BF)
            continue
        for order in range(groups):
            g = lax.rem(info_ref[2] + order, groups)
            acc = acc_s.at[order % 2]
            acc[0:m] = jnp.dot(b_s[0:m], p_s[unit, g].reshape(channels, width), preferred_element_type=F32)
            for h in range(halves):
                inner = slice(h * lanes, (h + 1) * lanes)
                cols = pl.ds(pl.multiple_of(g * width + h * lanes, lanes), lanes)
                squares = jnp.zeros((kept, lanes), F32)
                for s in range(phases):
                    v = acc[s * kept : (s + 1) * kept, inner] + x1_s[s, :, cols]
                    squares += v * v * live
                    t_s[...] = v
                    for k in range(slots):
                        o_s[pl.ds(k * frames * phases + s, frames, stride=phases), :] = t_s[
                            pl.ds(k, frames, stride=slots), :
                        ]
                t_s[...] = squares
                sums = sum(t_s[f * slots : (f + 1) * slots, :] for f in range(frames))
                share = near_ref.shape[2]
                for j in range(0, lanes // share, 2):
                    even = sums if j == 0 else pltpu.roll(sums, lanes - j * share, 1)
                    odd = pltpu.roll(sums, lanes - (j + 1) * share, 1)
                    chip = lax.div(g * (width // share) + h * (lanes // share) + j, 2)
                    near_ref[chip] = jnp.where(info_ref[3] == 0, even, odd)[:, :share]
                    far_ref[chip] = jnp.where(info_ref[3] == 0, odd, even)[:, :share]
                for k in range(slots):
                    dec_refs[order][k, :, inner] = o_s[k * frames * phases : (k + 1) * frames * phases, :].astype(BF)


def place_kernel(info_ref, *refs):
    pieces, out_ref = refs[:-1], refs[-1]
    slots, samples, _ = pieces[0].shape
    for k, piece in enumerate(pieces):
        r = lax.rem(info_ref[0] - k + len(pieces), len(pieces))
        at = pl.multiple_of(lax.div(r, 2) * samples, samples)
        out_ref[pl.ds(lax.rem(r, 2) * slots, slots), pl.ds(at, samples), :] = piece[...]


def cost(flops, moved):
    return pl.CostEstimate(flops=flops, bytes_accessed=moved, transcendentals=0)


def run_pack(first, second):
    n = first.shape[0]

    def pack_kernel(first_ref, second_ref, out_ref):
        out_ref[0:n] = first_ref[...]
        out_ref[n:] = second_ref[...]

    return pl.pallas_call(
        pack_kernel,
        out_shape=jax.ShapeDtypeStruct((n + second.shape[0], *first.shape[1:]), first.dtype),
        compiler_params=pltpu.CompilerParams(vmem_limit_bytes=VMEM // 4),
        cost_estimate=cost(0, 4 * (first.size + second.size)),
        name="pack",
    )(first, second)


def run_front(info, lat, w_in, freq, own, other, slots, chips):
    groups, frames, lanes = lat.shape
    c0 = w_in.shape[1]
    cols = own.shape[2]
    half = cols // 2
    rows = frames * slots
    pad = EDGE * slots
    window = rows // chips + 2 * pad
    reach = w_in.shape[0] // (lanes // 2) // 2
    whole = pl.BlockSpec(own.shape, lambda i: (0, 0, 0))
    return pl.pallas_call(
        functools.partial(front_kernel, slots),
        grid=(rows // ROW_CHUNK,),
        in_specs=[
            pl.BlockSpec(memory_space=pltpu.SMEM),
            pl.BlockSpec(lat.shape, lambda i: (0, 0, 0)),
            pl.BlockSpec(w_in.shape, lambda i: (0, 0)),
            pl.BlockSpec(freq.shape, lambda i: (0, 0)),
            whole,
            whole,
        ],
        out_specs=pl.BlockSpec((chips, window, half), lambda i: (0, 0, 0)),
        out_shape=jax.ShapeDtypeStruct((chips, window, half), BF),
        scratch_shapes=[
            pltpu.VMEM((c0, cols), BF),
            pltpu.VMEM((rows + (2 * reach + 2) * slots, lanes), F32),
            pltpu.VMEM((rows + 2 * reach * slots, lanes), F32),
            pltpu.VMEM((rows + 16, cols), F32),
            pltpu.VMEM((rows + 2 * pad, half), F32),
        ],
        compiler_params=pltpu.CompilerParams(vmem_limit_bytes=VMEM),
        cost_estimate=cost(2 * rows * c0 * (w_in.shape[0] + cols), 2 * w_in.size),
        name="front",
    )(info, lat, w_in, freq, own, other)


def run_activate(x, freq, slots, reach):
    phases, halves, groups, rows, lanes = x.shape
    channels = groups * halves * lanes
    return pl.pallas_call(
        functools.partial(activate_kernel, slots),
        out_shape=jax.ShapeDtypeStruct((phases + 2 * reach, rows, channels), BF),
        scratch_shapes=[pltpu.VMEM((phases, rows + 16, channels), F32)],
        compiler_params=pltpu.CompilerParams(vmem_limit_bytes=VMEM),
        cost_estimate=cost(20 * x.size, 6 * x.size),
        name="activate",
    )(x, freq)


def run_units(info, act, x, freq, weights, slots, devices):
    phases, halves, groups, rows, lanes = x.shape
    _, shards, kinds, depth, width = weights.shape
    units = freq.shape[0]
    taps = kinds // units - 1
    kept = rows - 2 * EDGE * slots
    channels = groups * width
    m = phases * kept
    reach = taps // 2 * 3 ** (units - 1)
    vmem = pl.BlockSpec(memory_space=pltpu.VMEM)
    return pl.pallas_call(
        functools.partial(units_kernel, slots),
        in_specs=[
            pl.BlockSpec(memory_space=pltpu.SMEM),
            vmem,
            vmem,
            vmem,
            pl.BlockSpec(memory_space=pl.ANY),
        ],
        out_specs=[vmem] * (groups + 2),
        out_shape=[
            *[jax.ShapeDtypeStruct((slots, m // slots, width), BF)] * groups,
            *[jax.ShapeDtypeStruct((devices // 2, slots, channels // devices), F32)] * 2,
        ],
        scratch_shapes=[
            pltpu.VMEM((units * groups, shards, taps, depth, width), BF),
            pltpu.VMEM((units, groups, shards, depth, width), BF),
            pltpu.VMEM((phases, rows + 16, channels), F32),
            pltpu.VMEM((phases + 2 * reach, kept, channels), BF),
            pltpu.VMEM((phases, kept, channels), F32),
            pltpu.VMEM((2, phases * rows, width), F32),
            pltpu.VMEM((phases * rows, channels), BF),
            pltpu.VMEM((kept, lanes), F32),
            pltpu.VMEM((m, lanes), F32),
            pltpu.SemaphoreType.DMA((units * groups,)),
            pltpu.SemaphoreType.DMA((units,)),
        ],
        compiler_params=pltpu.CompilerParams(vmem_limit_bytes=VMEM),
        cost_estimate=cost((phases * rows + m) * kinds * channels * channels, 2 * weights.size),
        name="units",
    )(info, act, x, freq, weights)


def run_place(place, pieces):
    slots, samples, width = pieces[0].shape
    vmem = pl.BlockSpec(memory_space=pltpu.VMEM)
    return pl.pallas_call(
        place_kernel,
        in_specs=[pl.BlockSpec(memory_space=pltpu.SMEM), *[vmem] * len(pieces)],
        out_specs=vmem,
        out_shape=jax.ShapeDtypeStruct((2 * slots, len(pieces) // 2 * samples, width), pieces[0].dtype),
        compiler_params=pltpu.CompilerParams(vmem_limit_bytes=VMEM // 4),
        cost_estimate=cost(0, 4 * len(pieces) * pieces[0].size),
        name="place",
    )(place, *pieces)


def freq_rows(alpha):
    return jnp.stack([alpha / math.pi, 1.0 / alpha], axis=-2)


def body(
    latent,
    dest,
    lengths,
    input_conv_weight,
    snake_entry_frequency,
    upsample_weight,
    snake_unit_frequency,
    dilated_conv_weight,
    pointwise_conv_weight,
):
    everyone = ("y", "x", "z", "c")
    blocks = ("x", "z", "y")
    ny, nx, nz, nc = (lax.axis_size(a) for a in everyone)
    iy, ix, iz, ic = (lax.axis_index(a) for a in everyone)
    chips = ny * nx * nz
    here_clips, here_frames, width_in = latent.shape
    clips = dest.shape[0]
    frames = here_frames * nx * nz * nc
    slots = clips // nc
    own_frames = frames // chips
    units, taps = dilated_conv_weight.shape[:2]
    upk, c1_local = upsample_weight.shape[1:]
    phases = upk // 2
    halves = nx * nz // phases
    lanes = c1_local // halves
    first_slot = ic * slots

    weights = run_pack(dilated_conv_weight.reshape(-1, *dilated_conv_weight.shape[2:]), pointwise_conv_weight)
    kinds = weights.shape[0]
    weights = lax.all_gather(weights, everyone, axis=0, tiled=True)
    weights = weights.reshape(ny, nx * nz * nc, kinds, *weights.shape[1:])

    packed = latent.transpose(1, 0, 2).reshape(here_frames, here_clips * width_in)
    packed = jnp.broadcast_to(packed[None], (ny * nx * nz * nc,) + packed.shape)
    packed = lax.all_to_all(packed, everyone, 0, 0, tiled=True)
    my_dest = lax.dynamic_slice_in_dim(dest, first_slot, slots)
    my_lengths = lax.dynamic_slice_in_dim(lengths, first_slot, slots)

    order = []
    for s in range(phases):
        near = s + phases // 2
        far = s + 3 * phases // 2 if s < phases // 2 else s - phases // 2
        order += [near, far]
    up = upsample_weight.transpose(1, 0, 2)
    up = jnp.stack([up[q] for q in order]).reshape(phases, 2, -1, halves, lanes)
    up = up.transpose(0, 3, 2, 1, 4).reshape(phases * halves, -1, 2 * lanes)
    up, packed = lax.optimization_barrier((up, packed))
    own = lax.all_to_all(up, ("x", "z"), 0, 0, tiled=True)
    other = lax.ppermute(own, "c", [(i, nc - 1 - i) for i in range(nc)])

    w_in = input_conv_weight.reshape(-1, input_conv_weight.shape[2])
    info = jnp.stack([ic, (ix * nz + iz) // (phases // 2 * halves)])
    info = jnp.concatenate([info, my_dest, my_lengths]).astype(jnp.int32)
    packed = packed.reshape(ny, frames, here_clips * width_in)
    x = run_front(info, packed, w_in, freq_rows(snake_entry_frequency), own, other, slots, chips)
    x = lax.all_to_all(x, blocks, 0, 0, tiled=True)
    x = x.reshape(phases, halves, ny, x.shape[1], lanes)

    freq = freq_rows(snake_unit_frequency).reshape(1, -1, c1_local)
    freq = lax.all_to_all(jnp.broadcast_to(freq, (ny,) + freq.shape[1:]), "y", 0, 0, tiled=True)
    freq = freq.transpose(1, 0, 2).reshape(units, -1, ny * c1_local)

    block = (ix * nz + iz) * ny + iy
    start = 2 * (iy % 2) + ic
    info = jnp.concatenate([jnp.stack([block * own_frames, frames, start, ic]), my_lengths]).astype(jnp.int32)
    act = run_activate(x, freq, slots, taps // 2)
    *decoded, near, far = run_units(info, act, x, freq, weights, slots, ny * nx * nz * nc)

    far = lax.ppermute(far, "c", [(i, nc - 1 - i) for i in range(nc)])
    squares = lax.all_to_all(jnp.concatenate([near, far], axis=1), ("y", "x", "z"), 0, 0, tiled=True)

    pieces = []
    for k, piece in enumerate(decoded):
        pairs = []
        for y in range(ny):
            for c in range(nc):
                target = (2 * (y % 2) + c + k) % ny
                pairs.append((y * nc + c, target * nc + y // 2))
        pieces.append(lax.ppermute(piece, ("y", "c"), pairs))
    decoded = run_place(iy[None].astype(jnp.int32), pieces)

    squares = squares.sum(axis=0)
    squares = jnp.where(ic == 0, squares, jnp.roll(squares, slots, axis=0))
    count = (phases * lengths[:, None]).astype(F32)
    energy = jnp.log(squares / count + 1e-06)
    return decoded, energy


def solution(mesh):
    ny = mesh.shape["clip"]
    side = 4
    fine = Mesh(mesh.devices.reshape(ny, side, side, 2), ("y", "x", "z", "c"))
    tm = ("x", "z", "c")
    in_specs = (
        P("y", tm, None),
        P(),
        P(),
        P(),
        P(),
        P(tm, None, "y"),
        P(None, None, "y"),
        P(None, None, tm, "y"),
        P(None, tm, "y"),
    )
    out_specs = (P(None, tm, "y"), P(None, ("y",) + tm))
    return jax.shard_map(body, mesh=fine, in_specs=in_specs, out_specs=out_specs, check_vma=False)
```

```python
import functools
import math

import jax
import jax.numpy as jnp
from jax import lax
from jax.experimental import pallas as pl
from jax.experimental.pallas import tpu as pltpu
from jax.sharding import Mesh
from jax.sharding import PartitionSpec as P

BF = jnp.bfloat16
F32 = jnp.float32
SIN2 = (
    9.869603157043457,
    -32.469581604003906,
    42.72538375854492,
    -30.085952758789062,
    12.990730285644531,
    -3.2729458808898926,
)
ROW_CHUNK = 512
EDGE = 2
VMEM = 60 * 1024 * 1024


def snake(value, turns, inverse):
    u = value * turns
    r = u - jnp.round(u)
    z = r * r
    p = jnp.full_like(z, SIN2[-1])
    for coefficient in SIN2[-2::-1]:
        p = p * z + coefficient
    return value + (p * z) * inverse


def front_kernel(slots, info_ref, lat_ref, w_in_ref, freq_ref, own_ref, other_ref, out_ref, w_s, one_s, two_s, prod_s, x_s):
    step, steps = pl.program_id(0), pl.num_programs(0)
    groups, depth, cols = own_ref.shape
    half = cols // 2
    _, frames, lanes = lat_ref.shape
    width = lanes // 2
    reach = w_in_ref.shape[0] // width // 2
    rows = frames * slots

    @pl.when(step == 0)
    def _():
        column = lax.broadcasted_iota(jnp.int32, (frames, lanes), 1)
        frame = lax.broadcasted_iota(jnp.int32, (frames, lanes), 0)
        edge = reach * slots
        one_s[0:edge, :] = jnp.zeros((edge, lanes), F32)
        one_s[edge + rows :, :] = jnp.zeros((one_s.shape[0] - edge - rows, lanes), F32)
        for k in range(slots):
            clip = info_ref[2 + k]
            v = lat_ref[lax.div(clip, 2)].astype(F32)
            v = jnp.where(lax.rem(clip, 2) == 1, pltpu.roll(v, width, 1), v)
            keep = (column < width) & (frame < info_ref[2 + slots + k])
            one_s[pl.ds(edge + k, frames, stride=slots), :] = jnp.where(keep, v, 0.0)
        total = two_s.shape[0]
        for r in range(0, total, ROW_CHUNK):
            size = min(ROW_CHUNK, total - r)
            after = pltpu.roll(one_s[r + slots : r + slots + size, :], width, 1)
            two_s[r : r + size, :] = one_s[r : r + size, :] + after

        first, second = (own_ref, other_ref), (other_ref, own_ref)
        for core, pair in enumerate((first, second)):

            @pl.when(info_ref[0] == core)
            def _(pair=pair):
                for g in range(groups):
                    for c in range(2):
                        w_s[(2 * g + c) * depth : (2 * g + c + 1) * depth, :] = pair[c][g]

        prod_s[0:8, :] = jnp.zeros((8, cols), F32)
        prod_s[prod_s.shape[0] - 8 :, :] = jnp.zeros((8, cols), F32)

    at = pl.multiple_of(step * ROW_CHUNK, ROW_CHUNK)
    taps = 2 * reach + 1
    lhs = []
    for t in range(0, taps, 2):
        v = two_s[pl.ds(pl.multiple_of(at + t * slots, 8), ROW_CHUNK), :].astype(BF)
        lhs.append(v if t + 1 < taps else v[:, :width])
    lhs = jnp.concatenate(lhs, axis=1)
    total = None
    block = 512
    for n in range(w_in_ref.shape[1] // block):
        part = slice(n * block, (n + 1) * block)
        pre = jnp.dot(lhs, w_in_ref[:, part], preferred_element_type=F32)
        s0 = snake(pre, freq_ref[0:1, part], freq_ref[1:2, part]).astype(BF)
        term = jnp.dot(s0, w_s[part, :], preferred_element_type=F32)
        total = term if total is None else total + term
    prod_s[pl.ds(pl.multiple_of(8 + at, 8), ROW_CHUNK), :] = total

    @pl.when(step == steps - 1)
    def _():
        pad = EDGE * slots
        x_s[0:pad, :] = jnp.zeros((pad, half), F32)
        x_s[x_s.shape[0] - pad :, :] = jnp.zeros((pad, half), F32)
        low = info_ref[1] == 0
        for r in range(0, rows, ROW_CHUNK):
            centre = prod_s[8 + r : 8 + r + ROW_CHUNK, :half]
            before = prod_s[8 - slots + r : 8 - slots + r + ROW_CHUNK, half:]
            after = prod_s[8 + slots + r : 8 + slots + r + ROW_CHUNK, half:]
            x_s[pad + r : pad + r + ROW_CHUNK, :] = centre + jnp.where(low, before, after)
        window = out_ref.shape[1]
        kept = window - 2 * pad
        for d in range(out_ref.shape[0]):
            out_ref[d] = x_s[d * kept : d * kept + window, :].astype(BF)


def activate_kernel(slots, x_ref, freq_ref, out_ref, act_s):
    phases, halves, groups, rows, lanes = x_ref.shape
    for s in range(phases):
        act_s[s, 0:8, :] = jnp.zeros((8, act_s.shape[2]), F32)
        act_s[s, 8 + rows :, :] = jnp.zeros((8, act_s.shape[2]), F32)
        for g in range(groups):
            for h in range(halves):
                cols = slice((g * halves + h) * lanes, (g * halves + h + 1) * lanes)
                v = x_ref[s, h, g].astype(F32)
                act_s[s, 8 : 8 + rows, cols] = snake(v, freq_ref[0, 0:1, cols], freq_ref[0, 1:2, cols])
    reach = (out_ref.shape[0] - phases) // 2
    for i in range(out_ref.shape[0]):
        n = i - reach
        at = 8 + n // phases * slots
        out_ref[i] = act_s[n % phases, at : at + rows, :].astype(BF)


def units_kernel(
    slots,
    info_ref,
    a0_ref,
    x_ref,
    freq_ref,
    w_ref,
    *refs,
):
    phases, halves, groups, rows, lanes = x_ref.shape
    dec_refs = refs[:groups]
    energy_ref, w_s, p_s, act_s, a1_s, x1_s, acc_s, b_s, t_s, o_s, w_sem, p_sem = refs[groups:]
    taps = w_s.shape[2]
    width = halves * lanes
    channels = groups * width
    first = EDGE * slots
    kept = rows - 2 * first
    frames = kept // slots
    units = w_sem.shape[0] // groups

    def fetch(unit):
        for g in range(groups):
            i = unit * groups + g
            yield pltpu.make_async_copy(w_ref.at[g, :, unit, 0:taps], w_s.at[i], w_sem.at[i])
        yield pltpu.make_async_copy(w_ref.at[:, :, unit, taps], p_s.at[unit], p_sem.at[unit])

    for copy in list(fetch(0))[: groups // 2]:
        copy.start()

    row = lax.broadcasted_iota(jnp.int32, (rows, lanes), 0)
    at = info_ref[0] - EDGE + (row >> (slots.bit_length() - 1))
    inside = jnp.where((at >= 0) & (at < info_ref[1]), 1.0, 0.0).astype(F32)
    row = lax.broadcasted_iota(jnp.int32, (kept, lanes), 0)
    at = info_ref[0] + (row >> (slots.bit_length() - 1))
    slot = row & (slots - 1)
    limit = jnp.zeros((kept, lanes), jnp.int32)
    for k in range(slots):
        limit = jnp.where(slot == k, info_ref[3 + k], limit)
    live = jnp.where(at < limit, 1.0, 0.0).astype(F32)

    for s in range(phases):
        act_s[s, 0:8, :] = jnp.zeros((8, channels), F32)
        act_s[s, 8 + rows :, :] = jnp.zeros((8, channels), F32)

    for unit in range(units):
        a_ref = a0_ref if unit == 0 else a1_s
        dilation = 3**unit
        m = phases * a_ref.shape[1]
        copies = list(fetch(unit))
        ahead = list(fetch(unit + 1)) if unit + 1 < units else []
        split = groups // 2 if unit == 0 else len(copies)
        for copy in copies[:split]:
            copy.wait()
        for copy in copies[split:] + ([] if unit == 0 else ahead):
            copy.start()
        for g in range(groups):
            if unit == 0 and g == split:
                for copy in copies[split:]:
                    copy.wait()
                for copy in ahead:
                    copy.start()
            total = None
            for t in range(taps):
                lhs = a_ref[dilation * t : dilation * t + phases].reshape(m, channels)
                rhs = w_s[unit * groups + g, :, t].reshape(channels, width)
                term = jnp.dot(lhs, rhs, preferred_element_type=F32)
                total = term if total is None else total + term
            acc_s[g % 2, 0:m] = total
            cols = slice(g * width, (g + 1) * width)
            b_s[0:m, cols] = snake(
                acc_s[g % 2, 0:m], freq_ref[unit, 2:3, cols], freq_ref[unit, 3:4, cols]
            ).astype(BF)
        if unit == 0:
            for g in range(groups):
                acc = acc_s.at[g % 2]
                acc[0:m] = jnp.dot(b_s[0:m], p_s[unit, g].reshape(channels, width), preferred_element_type=F32)
                for s in range(phases):
                    for h in range(halves):
                        cols = slice(g * width + h * lanes, g * width + (h + 1) * lanes)
                        v = acc[s * rows : (s + 1) * rows, h * lanes : (h + 1) * lanes]
                        v = v + x_ref[s, h, g].astype(F32)
                        x1_s[s, :, cols] = v[first : first + kept]
                        act_s[s, 8 : 8 + rows, cols] = (
                            snake(v, freq_ref[1, 0:1, cols], freq_ref[1, 1:2, cols]) * inside
                        )
            reach = (a1_s.shape[0] - phases) // 2
            for i in range(a1_s.shape[0]):
                n = i - reach
                at = 8 + first + n // phases * slots
                a1_s[i] = act_s[n % phases, at : at + kept, :].astype(BF)
            continue
        for order in range(groups):
            g = lax.rem(info_ref[2] + order, groups)
            acc = acc_s.at[order % 2]
            acc[0:m] = jnp.dot(b_s[0:m], p_s[unit, g].reshape(channels, width), preferred_element_type=F32)
            for h in range(halves):
                inner = slice(h * lanes, (h + 1) * lanes)
                cols = pl.ds(pl.multiple_of(g * width + h * lanes, lanes), lanes)
                squares = jnp.zeros((kept, lanes), F32)
                for s in range(phases):
                    v = acc[s * kept : (s + 1) * kept, inner] + x1_s[s, :, cols]
                    squares += v * v * live
                    t_s[...] = v
                    for k in range(slots):
                        o_s[pl.ds(k * frames * phases + s, frames, stride=phases), :] = t_s[
                            pl.ds(k, frames, stride=slots), :
                        ]
                t_s[...] = squares
                sums = sum(t_s[f * slots : (f + 1) * slots, :] for f in range(frames))
                share = energy_ref.shape[2]
                for j in range(lanes // share):
                    moved = sums if j == 0 else pltpu.roll(sums, lanes - j * share, 1)
                    energy_ref[g * (width // share) + h * (lanes // share) + j] = moved[:, :share]
                for k in range(slots):
                    dec_refs[order][k, :, inner] = o_s[k * frames * phases : (k + 1) * frames * phases, :].astype(BF)


def place_kernel(info_ref, *refs):
    pieces, out_ref = refs[:-1], refs[-1]
    slots, samples, _ = pieces[0].shape
    for k, piece in enumerate(pieces):
        r = lax.rem(info_ref[0] - k + len(pieces), len(pieces))
        at = pl.multiple_of(lax.div(r, 2) * samples, samples)
        out_ref[pl.ds(lax.rem(r, 2) * slots, slots), pl.ds(at, samples), :] = piece[...]


def cost(flops, moved):
    return pl.CostEstimate(flops=flops, bytes_accessed=moved, transcendentals=0)


def run_front(info, lat, w_in, freq, own, other, slots, chips):
    groups, frames, lanes = lat.shape
    c0 = w_in.shape[1]
    cols = own.shape[2]
    half = cols // 2
    rows = frames * slots
    pad = EDGE * slots
    window = rows // chips + 2 * pad
    reach = w_in.shape[0] // (lanes // 2) // 2
    whole = pl.BlockSpec(own.shape, lambda i: (0, 0, 0))
    return pl.pallas_call(
        functools.partial(front_kernel, slots),
        grid=(rows // ROW_CHUNK,),
        in_specs=[
            pl.BlockSpec(memory_space=pltpu.SMEM),
            pl.BlockSpec(lat.shape, lambda i: (0, 0, 0)),
            pl.BlockSpec(w_in.shape, lambda i: (0, 0)),
            pl.BlockSpec(freq.shape, lambda i: (0, 0)),
            whole,
            whole,
        ],
        out_specs=pl.BlockSpec((chips, window, half), lambda i: (0, 0, 0)),
        out_shape=jax.ShapeDtypeStruct((chips, window, half), BF),
        scratch_shapes=[
            pltpu.VMEM((c0, cols), BF),
            pltpu.VMEM((rows + (2 * reach + 2) * slots, lanes), F32),
            pltpu.VMEM((rows + 2 * reach * slots, lanes), F32),
            pltpu.VMEM((rows + 16, cols), F32),
            pltpu.VMEM((rows + 2 * pad, half), F32),
        ],
        compiler_params=pltpu.CompilerParams(vmem_limit_bytes=VMEM),
        cost_estimate=cost(2 * rows * c0 * (w_in.shape[0] + cols), 2 * w_in.size),
        name="front",
    )(info, lat, w_in, freq, own, other)


def run_activate(x, freq, slots, reach):
    phases, halves, groups, rows, lanes = x.shape
    channels = groups * halves * lanes
    return pl.pallas_call(
        functools.partial(activate_kernel, slots),
        out_shape=jax.ShapeDtypeStruct((phases + 2 * reach, rows, channels), BF),
        scratch_shapes=[pltpu.VMEM((phases, rows + 16, channels), F32)],
        compiler_params=pltpu.CompilerParams(vmem_limit_bytes=VMEM),
        cost_estimate=cost(20 * x.size, 6 * x.size),
        name="activate",
    )(x, freq)


def run_units(info, act, x, freq, weights, slots, devices):
    phases, halves, groups, rows, lanes = x.shape
    _, shards, units, kinds, depth, width = weights.shape
    taps = kinds - 1
    kept = rows - 2 * EDGE * slots
    channels = groups * width
    m = phases * kept
    reach = taps // 2 * 3 ** (units - 1)
    vmem = pl.BlockSpec(memory_space=pltpu.VMEM)
    return pl.pallas_call(
        functools.partial(units_kernel, slots),
        in_specs=[
            pl.BlockSpec(memory_space=pltpu.SMEM),
            vmem,
            vmem,
            vmem,
            pl.BlockSpec(memory_space=pl.ANY),
        ],
        out_specs=[vmem] * (groups + 1),
        out_shape=[
            *[jax.ShapeDtypeStruct((slots, m // slots, width), BF)] * groups,
            jax.ShapeDtypeStruct((devices, slots, channels // devices), F32),
        ],
        scratch_shapes=[
            pltpu.VMEM((units * groups, shards, taps, depth, width), BF),
            pltpu.VMEM((units, groups, shards, depth, width), BF),
            pltpu.VMEM((phases, rows + 16, channels), F32),
            pltpu.VMEM((phases + 2 * reach, kept, channels), BF),
            pltpu.VMEM((phases, kept, channels), F32),
            pltpu.VMEM((2, phases * rows, width), F32),
            pltpu.VMEM((phases * rows, channels), BF),
            pltpu.VMEM((kept, lanes), F32),
            pltpu.VMEM((m, lanes), F32),
            pltpu.SemaphoreType.DMA((units * groups,)),
            pltpu.SemaphoreType.DMA((units,)),
        ],
        compiler_params=pltpu.CompilerParams(vmem_limit_bytes=VMEM),
        cost_estimate=cost(2 * (phases * rows + m) * kinds * channels * channels, 2 * weights.size),
        name="units",
    )(info, act, x, freq, weights)


def run_place(place, pieces):
    slots, samples, width = pieces[0].shape
    vmem = pl.BlockSpec(memory_space=pltpu.VMEM)
    return pl.pallas_call(
        place_kernel,
        in_specs=[pl.BlockSpec(memory_space=pltpu.SMEM), *[vmem] * len(pieces)],
        out_specs=vmem,
        out_shape=jax.ShapeDtypeStruct((2 * slots, len(pieces) // 2 * samples, width), pieces[0].dtype),
        compiler_params=pltpu.CompilerParams(vmem_limit_bytes=VMEM // 4),
        cost_estimate=cost(0, 4 * len(pieces) * pieces[0].size),
        name="place",
    )(place, *pieces)


def freq_rows(alpha):
    return jnp.stack([alpha / math.pi, 1.0 / alpha], axis=-2)


def body(
    latent,
    dest,
    lengths,
    input_conv_weight,
    snake_entry_frequency,
    upsample_weight,
    snake_unit_frequency,
    dilated_conv_weight,
    pointwise_conv_weight,
):
    everyone = ("y", "x", "z", "c")
    blocks = ("x", "z", "y")
    ny, nx, nz, nc = (lax.axis_size(a) for a in everyone)
    iy, ix, iz, ic = (lax.axis_index(a) for a in everyone)
    chips = ny * nx * nz
    here_clips, here_frames, width_in = latent.shape
    clips = dest.shape[0]
    frames = here_frames * nx * nz * nc
    slots = clips // nc
    own_frames = frames // chips
    units, taps = dilated_conv_weight.shape[:2]
    upk, c1_local = upsample_weight.shape[1:]
    phases = upk // 2
    halves = nx * nz // phases
    lanes = c1_local // halves
    first_slot = ic * slots

    weights = jnp.concatenate([dilated_conv_weight, pointwise_conv_weight[:, None]], axis=1)
    shape = weights.shape
    weights = lax.all_gather(weights.reshape(-1, *shape[2:]), everyone, axis=0, tiled=True)
    weights = weights.reshape(ny, nx * nz * nc, *shape)

    packed = latent.transpose(1, 0, 2).reshape(here_frames, here_clips * width_in)
    packed = jnp.broadcast_to(packed[None], (ny * nx * nz * nc,) + packed.shape)
    packed = lax.all_to_all(packed, everyone, 0, 0, tiled=True)
    my_dest = lax.dynamic_slice_in_dim(dest, first_slot, slots)
    my_lengths = lax.dynamic_slice_in_dim(lengths, first_slot, slots)

    order = []
    for s in range(phases):
        near = s + phases // 2
        far = s + 3 * phases // 2 if s < phases // 2 else s - phases // 2
        order += [near, far]
    up = upsample_weight.transpose(1, 0, 2)
    up = jnp.stack([up[q] for q in order]).reshape(phases, 2, -1, halves, lanes)
    up = up.transpose(0, 3, 2, 1, 4).reshape(phases * halves, -1, 2 * lanes)
    up, packed = lax.optimization_barrier((up, packed))
    own = lax.all_to_all(up, ("x", "z"), 0, 0, tiled=True)
    other = lax.ppermute(own, "c", [(i, nc - 1 - i) for i in range(nc)])

    w_in = input_conv_weight.reshape(-1, input_conv_weight.shape[2])
    info = jnp.stack([ic, (ix * nz + iz) // (phases // 2 * halves)])
    info = jnp.concatenate([info, my_dest, my_lengths]).astype(jnp.int32)
    packed = packed.reshape(ny, frames, here_clips * width_in)
    x = run_front(info, packed, w_in, freq_rows(snake_entry_frequency), own, other, slots, chips)
    x, snake_unit_frequency = lax.optimization_barrier((x, snake_unit_frequency))
    x = lax.all_to_all(x, blocks, 0, 0, tiled=True)
    x = x.reshape(phases, halves, ny, x.shape[1], lanes)

    freq = freq_rows(snake_unit_frequency).reshape(1, -1, c1_local)
    freq = lax.all_to_all(jnp.broadcast_to(freq, (ny,) + freq.shape[1:]), "y", 0, 0, tiled=True)
    freq = freq.transpose(1, 0, 2).reshape(units, -1, ny * c1_local)

    block = (ix * nz + iz) * ny + iy
    start = 2 * (iy % 2) + ic
    info = jnp.concatenate([jnp.stack([block * own_frames, frames, start]), my_lengths]).astype(jnp.int32)
    act = run_activate(x, freq, slots, taps // 2)
    *decoded, squares = run_units(info, act, x, freq, weights, slots, ny * nx * nz * nc)

    squares = lax.all_to_all(squares, everyone, 0, 0, tiled=True)

    pieces = []
    for k, piece in enumerate(decoded):
        pairs = []
        for y in range(ny):
            for c in range(nc):
                target = (2 * (y % 2) + c + k) % ny
                pairs.append((y * nc + c, target * nc + y // 2))
        pieces.append(lax.ppermute(piece, ("y", "c"), pairs))
    decoded = run_place(iy[None].astype(jnp.int32), pieces)

    squares = squares.reshape(chips, clips, -1).sum(axis=0)
    count = (phases * lengths[:, None]).astype(F32)
    energy = jnp.log(squares / count + 1e-06)
    return decoded, energy


def solution(mesh):
    ny = mesh.shape["clip"]
    side = 4
    fine = Mesh(mesh.devices.reshape(ny, side, side, 2), ("y", "x", "z", "c"))
    tm = ("x", "z", "c")
    in_specs = (
        P("y", tm, None),
        P(),
        P(),
        P(),
        P(),
        P(tm, None, "y"),
        P(None, None, "y"),
        P(None, None, tm, "y"),
        P(None, tm, "y"),
    )
    out_specs = (P(None, tm, "y"), P(None, ("y",) + tm))
    return jax.shard_map(body, mesh=fine, in_specs=in_specs, out_specs=out_specs, check_vma=False)
```

```python
import functools
import math

import jax
import jax.numpy as jnp
from jax import lax
from jax.experimental import pallas as pl
from jax.experimental.pallas import tpu as pltpu
from jax.sharding import Mesh
from jax.sharding import PartitionSpec as P

BF = jnp.bfloat16
F32 = jnp.float32
SIN2 = (
    9.869603157043457,
    -32.469581604003906,
    42.72538375854492,
    -30.085952758789062,
    12.990730285644531,
    -3.2729458808898926,
)
ROW_CHUNK = 512
EDGE = 2
VMEM = 60 * 1024 * 1024


def snake(value, turns, inverse):
    u = value * turns
    r = u - jnp.round(u)
    z = r * r
    p = jnp.full_like(z, SIN2[-1])
    for coefficient in SIN2[-2::-1]:
        p = p * z + coefficient
    return value + (p * z) * inverse


def front_kernel(slots, info_ref, lat_ref, w_in_ref, freq_ref, own_ref, other_ref, out_ref, w_s, one_s, two_s, prod_s, x_s):
    step, steps = pl.program_id(0), pl.num_programs(0)
    groups, depth, cols = own_ref.shape
    half = cols // 2
    _, frames, lanes = lat_ref.shape
    width = lanes // 2
    reach = w_in_ref.shape[0] // width // 2
    rows = frames * slots

    @pl.when(step == 0)
    def _():
        column = lax.broadcasted_iota(jnp.int32, (frames, lanes), 1)
        frame = lax.broadcasted_iota(jnp.int32, (frames, lanes), 0)
        edge = reach * slots
        one_s[0:edge, :] = jnp.zeros((edge, lanes), F32)
        one_s[edge + rows :, :] = jnp.zeros((one_s.shape[0] - edge - rows, lanes), F32)
        for k in range(slots):
            clip = info_ref[2 + k]
            v = lat_ref[lax.div(clip, 2)].astype(F32)
            v = jnp.where(lax.rem(clip, 2) == 1, pltpu.roll(v, width, 1), v)
            keep = (column < width) & (frame < info_ref[2 + slots + k])
            one_s[pl.ds(edge + k, frames, stride=slots), :] = jnp.where(keep, v, 0.0)
        total = two_s.shape[0]
        for r in range(0, total, ROW_CHUNK):
            size = min(ROW_CHUNK, total - r)
            after = pltpu.roll(one_s[r + slots : r + slots + size, :], width, 1)
            two_s[r : r + size, :] = one_s[r : r + size, :] + after

        first, second = (own_ref, other_ref), (other_ref, own_ref)
        for core, pair in enumerate((first, second)):

            @pl.when(info_ref[0] == core)
            def _(pair=pair):
                for g in range(groups):
                    for c in range(2):
                        w_s[(2 * g + c) * depth : (2 * g + c + 1) * depth, :] = pair[c][g]

        prod_s[0:8, :] = jnp.zeros((8, cols), F32)
        prod_s[prod_s.shape[0] - 8 :, :] = jnp.zeros((8, cols), F32)

    at = pl.multiple_of(step * ROW_CHUNK, ROW_CHUNK)
    taps = 2 * reach + 1
    lhs = []
    for t in range(0, taps, 2):
        v = two_s[pl.ds(pl.multiple_of(at + t * slots, 8), ROW_CHUNK), :].astype(BF)
        lhs.append(v if t + 1 < taps else v[:, :width])
    lhs = jnp.concatenate(lhs, axis=1)
    total = None
    block = 512
    for n in range(w_in_ref.shape[1] // block):
        part = slice(n * block, (n + 1) * block)
        pre = jnp.dot(lhs, w_in_ref[:, part], preferred_element_type=F32)
        s0 = snake(pre, freq_ref[0:1, part], freq_ref[1:2, part]).astype(BF)
        term = jnp.dot(s0, w_s[part, :], preferred_element_type=F32)
        total = term if total is None else total + term
    prod_s[pl.ds(pl.multiple_of(8 + at, 8), ROW_CHUNK), :] = total

    @pl.when(step == steps - 1)
    def _():
        pad = EDGE * slots
        x_s[0:pad, :] = jnp.zeros((pad, half), F32)
        x_s[x_s.shape[0] - pad :, :] = jnp.zeros((pad, half), F32)
        low = info_ref[1] == 0
        for r in range(0, rows, ROW_CHUNK):
            centre = prod_s[8 + r : 8 + r + ROW_CHUNK, :half]
            before = prod_s[8 - slots + r : 8 - slots + r + ROW_CHUNK, half:]
            after = prod_s[8 + slots + r : 8 + slots + r + ROW_CHUNK, half:]
            x_s[pad + r : pad + r + ROW_CHUNK, :] = centre + jnp.where(low, before, after)
        window = out_ref.shape[1]
        kept = window - 2 * pad
        for d in range(out_ref.shape[0]):
            out_ref[d] = x_s[d * kept : d * kept + window, :].astype(BF)


def activate_kernel(slots, x_ref, freq_ref, out_ref, act_s):
    phases, halves, groups, rows, lanes = x_ref.shape
    for s in range(phases):
        act_s[s, 0:8, :] = jnp.zeros((8, act_s.shape[2]), F32)
        act_s[s, 8 + rows :, :] = jnp.zeros((8, act_s.shape[2]), F32)
        for g in range(groups):
            for h in range(halves):
                cols = slice((g * halves + h) * lanes, (g * halves + h + 1) * lanes)
                v = x_ref[s, h, g].astype(F32)
                act_s[s, 8 : 8 + rows, cols] = snake(v, freq_ref[0, 0:1, cols], freq_ref[0, 1:2, cols])
    reach = (out_ref.shape[0] - phases) // 2
    for i in range(out_ref.shape[0]):
        n = i - reach
        at = 8 + n // phases * slots
        out_ref[i] = act_s[n % phases, at : at + rows, :].astype(BF)


def units_kernel(
    slots,
    info_ref,
    a0_ref,
    x_ref,
    freq_ref,
    w_ref,
    *refs,
):
    phases, halves, groups, rows, lanes = x_ref.shape
    dec_refs = refs[:groups]
    energy_ref, w_s, p_s, act_s, a1_s, x1_s, acc_s, b_s, t_s, o_s, w_sem, p_sem = refs[groups:]
    taps = w_s.shape[2]
    width = halves * lanes
    channels = groups * width
    first = EDGE * slots
    kept = rows - 2 * first
    frames = kept // slots
    units = w_sem.shape[0] // groups

    def fetch(unit):
        for g in range(groups):
            i = unit * groups + g
            yield pltpu.make_async_copy(w_ref.at[g, :, unit, 0:taps], w_s.at[i], w_sem.at[i])
        yield pltpu.make_async_copy(w_ref.at[:, :, unit, taps], p_s.at[unit], p_sem.at[unit])

    for copy in list(fetch(0))[: groups // 2]:
        copy.start()

    row = lax.broadcasted_iota(jnp.int32, (rows, lanes), 0)
    at = info_ref[0] - EDGE + (row >> (slots.bit_length() - 1))
    inside = jnp.where((at >= 0) & (at < info_ref[1]), 1.0, 0.0).astype(F32)
    row = lax.broadcasted_iota(jnp.int32, (kept, lanes), 0)
    at = info_ref[0] + (row >> (slots.bit_length() - 1))
    slot = row & (slots - 1)
    limit = jnp.zeros((kept, lanes), jnp.int32)
    for k in range(slots):
        limit = jnp.where(slot == k, info_ref[3 + k], limit)
    live = jnp.where(at < limit, 1.0, 0.0).astype(F32)

    for s in range(phases):
        act_s[s, 0:8, :] = jnp.zeros((8, channels), F32)
        act_s[s, 8 + rows :, :] = jnp.zeros((8, channels), F32)

    for unit in range(units):
        a_ref = a0_ref if unit == 0 else a1_s
        dilation = 3**unit
        m = phases * a_ref.shape[1]
        copies = list(fetch(unit))
        ahead = list(fetch(unit + 1)) if unit + 1 < units else []
        split = groups // 2 if unit == 0 else len(copies)
        for copy in copies[:split]:
            copy.wait()
        for copy in copies[split:] + ([] if unit == 0 else ahead):
            copy.start()
        for g in range(groups):
            if unit == 0 and g == split:
                for copy in copies[split:]:
                    copy.wait()
                for copy in ahead:
                    copy.start()
            total = None
            for t in range(taps):
                lhs = a_ref[dilation * t : dilation * t + phases].reshape(m, channels)
                rhs = w_s[unit * groups + g, :, t].reshape(channels, width)
                term = jnp.dot(lhs, rhs, preferred_element_type=F32)
                total = term if total is None else total + term
            acc_s[g % 2, 0:m] = total
            cols = slice(g * width, (g + 1) * width)
            b_s[0:m, cols] = snake(
                acc_s[g % 2, 0:m], freq_ref[unit, 2:3, cols], freq_ref[unit, 3:4, cols]
            ).astype(BF)
        if unit == 0:
            for g in range(groups):
                acc = acc_s.at[g % 2]
                acc[0:m] = jnp.dot(b_s[0:m], p_s[unit, g].reshape(channels, width), preferred_element_type=F32)
                for s in range(phases):
                    for h in range(halves):
                        cols = slice(g * width + h * lanes, g * width + (h + 1) * lanes)
                        v = acc[s * rows : (s + 1) * rows, h * lanes : (h + 1) * lanes]
                        v = v + x_ref[s, h, g].astype(F32)
                        x1_s[s, :, cols] = v[first : first + kept]
                        act_s[s, 8 : 8 + rows, cols] = (
                            snake(v, freq_ref[1, 0:1, cols], freq_ref[1, 1:2, cols]) * inside
                        )
            reach = (a1_s.shape[0] - phases) // 2
            for i in range(a1_s.shape[0]):
                n = i - reach
                at = 8 + first + n // phases * slots
                a1_s[i] = act_s[n % phases, at : at + kept, :].astype(BF)
            continue
        for order in range(groups):
            g = lax.rem(info_ref[2] + order, groups)
            acc = acc_s.at[order % 2]
            acc[0:m] = jnp.dot(b_s[0:m], p_s[unit, g].reshape(channels, width), preferred_element_type=F32)
            for h in range(halves):
                inner = slice(h * lanes, (h + 1) * lanes)
                cols = pl.ds(pl.multiple_of(g * width + h * lanes, lanes), lanes)
                squares = jnp.zeros((kept, lanes), F32)
                for s in range(phases):
                    v = acc[s * kept : (s + 1) * kept, inner] + x1_s[s, :, cols]
                    squares += v * v * live
                    t_s[...] = v
                    for k in range(slots):
                        o_s[pl.ds(k * frames * phases + s, frames, stride=phases), :] = t_s[
                            pl.ds(k, frames, stride=slots), :
                        ]
                t_s[...] = squares
                sums = sum(t_s[f * slots : (f + 1) * slots, :] for f in range(frames))
                share = energy_ref.shape[2]
                for j in range(lanes // share):
                    moved = sums if j == 0 else pltpu.roll(sums, lanes - j * share, 1)
                    energy_ref[g * (width // share) + h * (lanes // share) + j] = moved[:, :share]
                for k in range(slots):
                    dec_refs[order][k, :, inner] = o_s[k * frames * phases : (k + 1) * frames * phases, :].astype(BF)


def place_kernel(info_ref, *refs):
    pieces, out_ref = refs[:-1], refs[-1]
    slots, samples, _ = pieces[0].shape
    for k, piece in enumerate(pieces):
        r = lax.rem(info_ref[0] - k + len(pieces), len(pieces))
        at = pl.multiple_of(lax.div(r, 2) * samples, samples)
        out_ref[pl.ds(lax.rem(r, 2) * slots, slots), pl.ds(at, samples), :] = piece[...]


def cost(flops, moved):
    return pl.CostEstimate(flops=flops, bytes_accessed=moved, transcendentals=0)


def run_front(info, lat, w_in, freq, own, other, slots, chips):
    groups, frames, lanes = lat.shape
    c0 = w_in.shape[1]
    cols = own.shape[2]
    half = cols // 2
    rows = frames * slots
    pad = EDGE * slots
    window = rows // chips + 2 * pad
    reach = w_in.shape[0] // (lanes // 2) // 2
    whole = pl.BlockSpec(own.shape, lambda i: (0, 0, 0))
    return pl.pallas_call(
        functools.partial(front_kernel, slots),
        grid=(rows // ROW_CHUNK,),
        in_specs=[
            pl.BlockSpec(memory_space=pltpu.SMEM),
            pl.BlockSpec(lat.shape, lambda i: (0, 0, 0)),
            pl.BlockSpec(w_in.shape, lambda i: (0, 0)),
            pl.BlockSpec(freq.shape, lambda i: (0, 0)),
            whole,
            whole,
        ],
        out_specs=pl.BlockSpec((chips, window, half), lambda i: (0, 0, 0)),
        out_shape=jax.ShapeDtypeStruct((chips, window, half), BF),
        scratch_shapes=[
            pltpu.VMEM((c0, cols), BF),
            pltpu.VMEM((rows + (2 * reach + 2) * slots, lanes), F32),
            pltpu.VMEM((rows + 2 * reach * slots, lanes), F32),
            pltpu.VMEM((rows + 16, cols), F32),
            pltpu.VMEM((rows + 2 * pad, half), F32),
        ],
        compiler_params=pltpu.CompilerParams(vmem_limit_bytes=VMEM),
        cost_estimate=cost(2 * rows * c0 * (w_in.shape[0] + cols), 2 * w_in.size),
        name="front",
    )(info, lat, w_in, freq, own, other)


def run_activate(x, freq, slots, reach):
    phases, halves, groups, rows, lanes = x.shape
    channels = groups * halves * lanes
    return pl.pallas_call(
        functools.partial(activate_kernel, slots),
        out_shape=jax.ShapeDtypeStruct((phases + 2 * reach, rows, channels), BF),
        scratch_shapes=[pltpu.VMEM((phases, rows + 16, channels), F32)],
        compiler_params=pltpu.CompilerParams(vmem_limit_bytes=VMEM),
        cost_estimate=cost(20 * x.size, 6 * x.size),
        name="activate",
    )(x, freq)


def run_units(info, act, x, freq, weights, slots, devices):
    phases, halves, groups, rows, lanes = x.shape
    _, shards, units, kinds, depth, width = weights.shape
    taps = kinds - 1
    kept = rows - 2 * EDGE * slots
    channels = groups * width
    m = phases * kept
    reach = taps // 2 * 3 ** (units - 1)
    vmem = pl.BlockSpec(memory_space=pltpu.VMEM)
    return pl.pallas_call(
        functools.partial(units_kernel, slots),
        in_specs=[
            pl.BlockSpec(memory_space=pltpu.SMEM),
            vmem,
            vmem,
            vmem,
            pl.BlockSpec(memory_space=pl.ANY),
        ],
        out_specs=[vmem] * (groups + 1),
        out_shape=[
            *[jax.ShapeDtypeStruct((slots, m // slots, width), BF)] * groups,
            jax.ShapeDtypeStruct((devices, slots, channels // devices), F32),
        ],
        scratch_shapes=[
            pltpu.VMEM((units * groups, shards, taps, depth, width), BF),
            pltpu.VMEM((units, groups, shards, depth, width), BF),
            pltpu.VMEM((phases, rows + 16, channels), F32),
            pltpu.VMEM((phases + 2 * reach, kept, channels), BF),
            pltpu.VMEM((phases, kept, channels), F32),
            pltpu.VMEM((2, phases * rows, width), F32),
            pltpu.VMEM((phases * rows, channels), BF),
            pltpu.VMEM((kept, lanes), F32),
            pltpu.VMEM((m, lanes), F32),
            pltpu.SemaphoreType.DMA((units * groups,)),
            pltpu.SemaphoreType.DMA((units,)),
        ],
        compiler_params=pltpu.CompilerParams(vmem_limit_bytes=VMEM),
        cost_estimate=cost(2 * (phases * rows + m) * kinds * channels * channels, 2 * weights.size),
        name="units",
    )(info, act, x, freq, weights)


def run_place(place, pieces):
    slots, samples, width = pieces[0].shape
    vmem = pl.BlockSpec(memory_space=pltpu.VMEM)
    return pl.pallas_call(
        place_kernel,
        in_specs=[pl.BlockSpec(memory_space=pltpu.SMEM), *[vmem] * len(pieces)],
        out_specs=vmem,
        out_shape=jax.ShapeDtypeStruct((2 * slots, len(pieces) // 2 * samples, width), pieces[0].dtype),
        compiler_params=pltpu.CompilerParams(vmem_limit_bytes=VMEM // 4),
        cost_estimate=cost(0, 4 * len(pieces) * pieces[0].size),
        name="place",
    )(place, *pieces)


def freq_rows(alpha):
    return jnp.stack([alpha / math.pi, 1.0 / alpha], axis=-2)


def body(
    latent,
    dest,
    lengths,
    input_conv_weight,
    snake_entry_frequency,
    upsample_weight,
    snake_unit_frequency,
    dilated_conv_weight,
    pointwise_conv_weight,
):
    everyone = ("y", "x", "z", "c")
    blocks = ("x", "z", "y")
    ny, nx, nz, nc = (lax.axis_size(a) for a in everyone)
    iy, ix, iz, ic = (lax.axis_index(a) for a in everyone)
    chips = ny * nx * nz
    here_clips, here_frames, width_in = latent.shape
    clips = dest.shape[0]
    frames = here_frames * nx * nz * nc
    slots = clips // nc
    own_frames = frames // chips
    units, taps = dilated_conv_weight.shape[:2]
    upk, c1_local = upsample_weight.shape[1:]
    phases = upk // 2
    halves = nx * nz // phases
    lanes = c1_local // halves
    first_slot = ic * slots

    weights = jnp.concatenate([dilated_conv_weight, pointwise_conv_weight[:, None]], axis=1)
    shape = weights.shape
    weights = lax.all_gather(weights.reshape(-1, *shape[2:]), everyone, axis=0, tiled=True)
    weights = weights.reshape(ny, nx * nz * nc, *shape)

    packed = latent.transpose(1, 0, 2).reshape(here_frames, here_clips * width_in)
    packed = jnp.broadcast_to(packed[None], (ny * nx * nz * nc,) + packed.shape)
    packed = lax.all_to_all(packed, everyone, 0, 0, tiled=True)
    my_dest = lax.dynamic_slice_in_dim(dest, first_slot, slots)
    my_lengths = lax.dynamic_slice_in_dim(lengths, first_slot, slots)

    order = []
    for s in range(phases):
        near = s + phases // 2
        far = s + 3 * phases // 2 if s < phases // 2 else s - phases // 2
        order += [near, far]
    up = upsample_weight.transpose(1, 0, 2)
    up = jnp.stack([up[q] for q in order]).reshape(phases, 2, -1, halves, lanes)
    up = up.transpose(0, 3, 2, 1, 4).reshape(phases * halves, -1, 2 * lanes)
    up, packed = lax.optimization_barrier((up, packed))
    own = lax.all_to_all(up, ("x", "z"), 0, 0, tiled=True)
    other = lax.ppermute(own, "c", [(i, nc - 1 - i) for i in range(nc)])

    w_in = input_conv_weight.reshape(-1, input_conv_weight.shape[2])
    info = jnp.stack([ic, (ix * nz + iz) // (phases // 2 * halves)])
    info = jnp.concatenate([info, my_dest, my_lengths]).astype(jnp.int32)
    packed = packed.reshape(ny, frames, here_clips * width_in)
    x = run_front(info, packed, w_in, freq_rows(snake_entry_frequency), own, other, slots, chips)
    x = lax.all_to_all(x, blocks, 0, 0, tiled=True)
    x, snake_unit_frequency = lax.optimization_barrier((x, snake_unit_frequency))
    x = x.reshape(phases, halves, ny, x.shape[1], lanes)

    freq = freq_rows(snake_unit_frequency).reshape(1, -1, c1_local)
    freq = lax.all_to_all(jnp.broadcast_to(freq, (ny,) + freq.shape[1:]), "y", 0, 0, tiled=True)
    freq = freq.transpose(1, 0, 2).reshape(units, -1, ny * c1_local)

    block = (ix * nz + iz) * ny + iy
    start = 2 * (iy % 2) + ic
    info = jnp.concatenate([jnp.stack([block * own_frames, frames, start]), my_lengths]).astype(jnp.int32)
    act = run_activate(x, freq, slots, taps // 2)
    *decoded, squares = run_units(info, act, x, freq, weights, slots, ny * nx * nz * nc)

    squares = lax.all_to_all(squares, everyone, 0, 0, tiled=True)

    pieces = []
    for k, piece in enumerate(decoded):
        pairs = []
        for y in range(ny):
            for c in range(nc):
                target = (2 * (y % 2) + c + k) % ny
                pairs.append((y * nc + c, target * nc + y // 2))
        pieces.append(lax.ppermute(piece, ("y", "c"), pairs))
    decoded = run_place(iy[None].astype(jnp.int32), pieces)

    squares = squares.reshape(chips, clips, -1).sum(axis=0)
    count = (phases * lengths[:, None]).astype(F32)
    energy = jnp.log(squares / count + 1e-06)
    return decoded, energy


def solution(mesh):
    ny = mesh.shape["clip"]
    side = 4
    fine = Mesh(mesh.devices.reshape(ny, side, side, 2), ("y", "x", "z", "c"))
    tm = ("x", "z", "c")
    in_specs = (
        P("y", tm, None),
        P(),
        P(),
        P(),
        P(),
        P(tm, None, "y"),
        P(None, None, "y"),
        P(None, None, tm, "y"),
        P(None, tm, "y"),
    )
    out_specs = (P(None, tm, "y"), P(None, ("y",) + tm))
    return jax.shard_map(body, mesh=fine, in_specs=in_specs, out_specs=out_specs, check_vma=False)
```
